32 devices in a mesh: ens: 2 (over y), patch: 4 (over z), mp: 4 (over x, core).
Axes of the slice: x: 2, y: 2, z: 4, core: 2. Of those that a mesh axis runs over, the one named last changes fastest.
Arguments:
- grid_in: bfloat16 [84, 4096], P(None, ('ens', 'patch')), parts along dimension 1, may hold values from -6 to 6
- mesh_static: bfloat16 [1024, 512], P('patch'), may hold values from -50 to 50
- embed_weight: bfloat16 [84, 512], replicated, may hold values from -0.625 to 0.625
- embed_bias: float32 [512], replicated, may hold values from -3 to 3
- encode_source: bfloat16 [512, 512], P(None, 'mp'), may hold values from -0.25 to 0.25
- encode_target: bfloat16 [512, 512], P(None, 'mp'), may hold values from -0.25 to 0.25
- encode_edge: bfloat16 [4, 512], P(None, 'mp'), may hold values from -3 to 3
- encode_bias: float32 [512], P('mp'), may hold values from -3 to 3
- encode_out: bfloat16 [512, 512], P('mp'), may hold values from -0.125 to 0.125
- layer_gain: float32 [2, 512], replicated, may hold values from 0.5 to 1.5
- attention_in: bfloat16 [2, 512, 3, 512], P(None, None, None, 'mp'), may hold values from -0.25 to 0.25
- query_gain: float32 [2, 128], replicated, may hold values from 0.5 to 2.5
- key_gain: float32 [2, 128], replicated, may hold values from 0.5 to 2.5
- attention_out: bfloat16 [2, 512, 512], P(None, 'mp'), may hold values from -0.25 to 0.25
- hidden_in: bfloat16 [2, 512, 2048], P(None, None, 'mp'), may hold values from -0.25 to 0.25
- hidden_out: bfloat16 [2, 2048, 512], P(None, 'mp'), may hold values from -0.125 to 0.125
- final_gain: float32 [512], replicated, may hold values from 0.5 to 1.5
- decode_node: bfloat16 [512, 512], P(None, 'mp'), may hold values from -0.25 to 0.25
- decode_grid: bfloat16 [512, 512], P(None, 'mp'), may hold values from -0.25 to 0.25
- decode_bias: float32 [512], P('mp'), may hold values from -3 to 3
- decode_out: bfloat16 [512, 84], P('mp'), may hold values from -0.25 to 0.25
- cell_lists: int32 [4, 4, 256], P('patch'), may hold values from 0 to 511
- edge_source: int32 [4, 1024], P('patch'), may hold values from 0 to 1535, as said below
- edge_target: int32 [4, 1024], P('patch'), may hold values from 0 to 256, as said below
- edge_geometry: bfloat16 [4, 4, 1024], P('patch'), may hold values from -6 to 6
- halo_lists: int32 [4, 4, 128], P('patch'), may hold values from 0 to 255
- neighbours: int32 [4, 32, 256], P('patch'), may hold values from 0 to 767, as said below
- node_lists: int32 [4, 4, 128], P('patch'), may hold values from 0 to 255
- cell_nodes: int32 [3, 2048], P(None, 'patch'), may hold values from 0 to 767, as said below
Outputs:
- denoised: bfloat16 [84, 4096], P(None, ('ens', 'patch')), parts along dimension 1
The draws below stay inside these ranges and needn't reach their ends.
There are 2 independent parts, one for each index of `ens`. The reference program is written for one: setup_inputs(seed, part) draws one part's arguments, and reference() takes and returns one part's arrays. A program takes and returns all parts, laid end to end along the dimension named above; an argument that names none is the same for every part. Nothing has to cross between parts.
Inputs may be any that keep to these rules, and one draw needn't show every extreme that they name: `cell_lists`: entry [p, k, j] is a cell of band p, numbered within the band, sent as row j of band p's list for patch p + b_k; entries may repeat. `edge_source`: entry [p, e] is the sender row of edge slot e of patch p in cell_table_p: below 512 a cell of band p, else row 512 + k * 256 + j, entry j of the list that band p - b_k sends; never a list of a band beyond the ends. `edge_target`: entry [p, e] is the receiving node of edge slot e of patch p, numbered within the patch; 256 marks padding, which stands only after all real edges of the patch; real receivers ascend along a patch's row; the first and the last patch have no padding. `halo_lists`: entry [p, k, j] is a node of patch p sent as row j of its key list for patch p + b_k; entries may repeat. `neighbours`: entry [p, n, i] is the n-th key of node i of patch p in key_table_p: below 256 a node of patch p, else row 256 + k * 128 + j, entry j of the key list that patch p - b_k sends; never a list of a patch beyond the ends; keys may repeat. `node_lists`: entry [p, k, j] is a node of patch p sent as row j of its decoder list for band p + b_k; entries may repeat. `cell_nodes`: entry [j, g] is a row of node_table_p for the band p of cell g: below 256 a node of patch p, else row 256 + k * 128 + i, entry i of the decoder list that patch p - b_k sends; never a list of a patch beyond the ends.
All inputs are finite; a program needn't handle non-finite values.
Results may differ from the reference program's by a relative error of at most 0.02.
Values may be sent and summed in bfloat16 or wider, within the bound.
A program may use at most 64 MiB of HBM per device.

```python
import math
import jax
import jax.numpy as jnp
from jax import lax

D = 512
FF = 2048
CH = 84
HEADS = 4
HEAD = 128
EFEAT = 4
LAYERS = 2
REACH = 2
NBR = 32
G_DEV = 512
M_DEV = 256
E_G2M = 1024
CAP_G = 256
CAP_H = 128
CAP_D = 128
PATCHES = 4
GRID = 2048
MESH = 1024
N_MP = 4


def block_offset(number):
    return (number // 2 + 1) * (1 - 2 * (number % 2))


def table_draw(key, patch_ids, local_rows, capacity):
    choose_key, local_key, near_key = jax.random.split(key, 3)
    chooser = jax.random.randint(choose_key, patch_ids.shape, 0, 2 * REACH + 2)
    number = chooser - 2
    source = patch_ids - block_offset(jnp.maximum(number, 0))
    usable = (number >= 0) & (source >= 0) & (source < PATCHES)
    local_pick = jax.random.randint(local_key, patch_ids.shape, 0, local_rows)
    near_pick = jax.random.randint(near_key, patch_ids.shape, 0, capacity)
    return jnp.where(usable, local_rows + jnp.maximum(number, 0) * capacity + near_pick, local_pick).astype(jnp.int32)


def draw_edge_source(key, part):
    key = jax.random.fold_in(key, 1)
    order_key, local_key = jax.random.split(key, 2)
    total_rows = G_DEV + 2 * REACH * CAP_G
    row_keys = jax.random.split(order_key, PATCHES)
    order = jax.vmap(lambda row_key: jax.random.permutation(row_key, total_rows))(row_keys)[:, :E_G2M].astype(jnp.int32)
    patch_ids = lax.broadcasted_iota(jnp.int32, (PATCHES, E_G2M), 0)
    number = jnp.maximum(order - G_DEV, 0) // CAP_G
    source = patch_ids - block_offset(number)
    usable = (order < G_DEV) | (source >= 0) & (source < PATCHES)
    local_pick = jax.random.randint(local_key, (PATCHES, E_G2M), 0, G_DEV)
    drawn = jnp.where(usable, order, local_pick).astype(jnp.int32)
    drawn = drawn.at[0, 0].set(G_DEV + 2 * REACH * CAP_G - 1)
    return drawn.at[0, 1].set(0)


def draw_edge_target(key, part):
    key = jax.random.fold_in(key, 2)
    count_key, node_key = jax.random.split(key, 2)
    patch_ids = lax.broadcasted_iota(jnp.int32, (PATCHES,), 0)
    counts = jax.random.randint(count_key, (PATCHES,), 7 * E_G2M // 8, E_G2M + 1)
    polar = (patch_ids == 0) | (patch_ids == PATCHES - 1)
    counts = jnp.where(polar, E_G2M, counts)
    nodes = jax.random.randint(node_key, (PATCHES, E_G2M), 0, M_DEV)
    position = lax.broadcasted_iota(jnp.int32, (PATCHES, E_G2M), 1)
    nodes = jnp.where(position < counts[:, None], nodes, M_DEV)
    nodes = nodes.at[0, 0].set(0)
    return jnp.sort(nodes, axis=1).astype(jnp.int32)


def draw_neighbours(key, part):
    key = jax.random.fold_in(key, 3)
    patch_ids = lax.broadcasted_iota(jnp.int32, (PATCHES, NBR, M_DEV), 0)
    drawn = table_draw(key, patch_ids, M_DEV, CAP_H)
    drawn = drawn.at[0, 0, 0].set(M_DEV + 2 * REACH * CAP_H - 1)
    return drawn.at[0, 0, 1].set(0)


def draw_cell_nodes(key, part):
    key = jax.random.fold_in(key, 4)
    patch_ids = lax.broadcasted_iota(jnp.int32, (3, GRID), 1) // G_DEV
    drawn = table_draw(key, patch_ids, M_DEV, CAP_D)
    drawn = drawn.at[0, 0].set(M_DEV + 2 * REACH * CAP_D - 1)
    return drawn.at[0, 1].set(0)


def draw_mesh_static(key, part):
    key = jax.random.fold_in(key, 5)
    row_key, column_key, value_key = jax.random.split(key, 3)
    row_scale = jnp.exp(jax.random.uniform(row_key, (MESH, 1), minval=-1.15, maxval=1.15))
    column_scale = jnp.exp(jax.random.uniform(column_key, (1, D), minval=-1.15, maxval=1.15))
    values = jnp.clip(jax.random.normal(value_key, (MESH, D)), -5.0, 5.0)
    return (values * row_scale * column_scale).astype(jnp.bfloat16)


def touch_ends(result, rng, least, high):
    longest = result.shape.index(max(result.shape))
    spots = []
    for shift in (0, 1):
        where = [jax.random.randint(jax.random.fold_in(rng, axis), (), 0, length) for axis, length in enumerate(result.shape)]
        where[longest] = (where[longest] + shift) % result.shape[longest]
        spots.append(tuple(where))
    return result.at[spots[0]].set(least).at[spots[1]].set(high)


def steps_of(own_key, extent, cuts, low, top_value):
    def one(axis_at, parts):
        draws = jax.random.uniform(jax.random.fold_in(jax.random.fold_in(own_key, 6), axis_at), (parts,), jnp.float32, low / len(cuts), top_value / len(cuts))
        return jnp.repeat(jnp.exp(draws), extent[axis_at] // parts).reshape((-1,) + (1,) * (len(extent) - axis_at - 1))

    level = one(*cuts[0])
    for cut in cuts[1:]:
        level = level * one(*cut)
    return level


def scatter_about(rng, dims, scale, most, cuts=(), kind=jnp.bfloat16):
    values = jax.random.normal(rng, dims, jnp.float32) * scale
    if len(cuts) > 0:
        values = steps_of(rng, dims, cuts, -0.22, 0.18) * values
    return jnp.clip(values, min=-most, max=most).astype(kind)


def setup_inputs(seed: int = 0, part: int = 0) -> dict:
    splits = jax.random.split(jax.random.key(seed), 30)
    part_splits = jax.random.split(jax.random.fold_in(splits[29], part), 30)
    return {
        "grid_in": scatter_about(part_splits[0], (CH, GRID), 1.0, 6.0, ((1, 4),)),
        "mesh_static": draw_mesh_static(jax.random.fold_in(splits[29], 71), part),
        "embed_weight": scatter_about(splits[2], (CH, D), CH ** -0.5, 0.625),
        "embed_bias": scatter_about(splits[3], (D,), 0.5, 3.0, (), jnp.float32),
        "encode_source": scatter_about(splits[4], (D, D), D ** -0.5, 0.25, ((1, 4),)),
        "encode_target": scatter_about(splits[5], (D, D), D ** -0.5, 0.25, ((1, 4),)),
        "encode_edge": scatter_about(splits[6], (EFEAT, D), EFEAT ** -0.5, 3.0, ((1, 4),)),
        "encode_bias": scatter_about(splits[7], (D,), 0.5, 3.0, ((0, 4),), jnp.float32),
        "encode_out": scatter_about(splits[8], (D, D), (D * E_G2M // M_DEV) ** -0.5, 0.125, ((0, 4),)),
        "layer_gain": jnp.clip(1.0 + 0.1 * jax.random.normal(splits[9], (LAYERS, D), jnp.float32), 0.5, 1.5),
        "attention_in": scatter_about(splits[10], (LAYERS, D, 3, D), D ** -0.5, 0.25, ((3, 4),)),
        "query_gain": jnp.clip(jnp.exp(jax.random.uniform(splits[11], (LAYERS, HEAD), jnp.float32, math.log(0.5), math.log(2.5))), 0.5, 2.5),
        "key_gain": jnp.clip(jnp.exp(jax.random.uniform(splits[12], (LAYERS, HEAD), jnp.float32, math.log(0.5), math.log(2.5))), 0.5, 2.5),
        "attention_out": scatter_about(splits[13], (LAYERS, D, D), D ** -0.5, 0.25, ((1, 4),)),
        "hidden_in": scatter_about(splits[14], (LAYERS, D, FF), D ** -0.5, 0.25, ((2, 4),)),
        "hidden_out": scatter_about(splits[15], (LAYERS, FF, D), FF ** -0.5, 0.125, ((1, 4),)),
        "final_gain": jnp.clip(1.0 + 0.1 * jax.random.normal(splits[16], (D,), jnp.float32), 0.5, 1.5),
        "decode_node": scatter_about(splits[17], (D, D), D ** -0.5, 0.25, ((1, 4),)),
        "decode_grid": scatter_about(splits[18], (D, D), D ** -0.5, 0.25, ((1, 4),)),
        "decode_bias": scatter_about(splits[19], (D,), 0.5, 3.0, ((0, 4),), jnp.float32),
        "decode_out": scatter_about(splits[20], (D, CH), D ** -0.5, 0.25, ((0, 4),)),
        "cell_lists": touch_ends(jax.random.randint(splits[21], (PATCHES, 2 * REACH, CAP_G), 0, G_DEV), jax.random.fold_in(splits[21], 1), 0, G_DEV - 1).astype(jnp.int32),
        "edge_source": draw_edge_source(jax.random.fold_in(splits[29], 71), part),
        "edge_target": draw_edge_target(jax.random.fold_in(splits[29], 71), part),
        "edge_geometry": scatter_about(splits[24], (PATCHES, EFEAT, E_G2M), 1.0, 6.0, ((0, 4),)),
        "halo_lists": touch_ends(jax.random.randint(splits[25], (PATCHES, 2 * REACH, CAP_H), 0, M_DEV), jax.random.fold_in(splits[25], 1), 0, M_DEV - 1).astype(jnp.int32),
        "neighbours": draw_neighbours(jax.random.fold_in(splits[29], 71), part),
        "node_lists": touch_ends(jax.random.randint(splits[27], (PATCHES, 2 * REACH, CAP_D), 0, M_DEV), jax.random.fold_in(splits[27], 1), 0, M_DEV - 1).astype(jnp.int32),
        "cell_nodes": draw_cell_nodes(jax.random.fold_in(splits[29], 71), part),
    }


norm_epsilon = 1e-05

def offset_of(number):
    return (number // 2 + 1) * (1 if number % 2 == 0 else -1)

def layer_norm(values, norm_gain):
    average = lax.optimization_barrier(jnp.mean(values, axis=-1, keepdims=True))
    centred = values - average
    spread = lax.optimization_barrier(jnp.mean(centred * centred, axis=-1, keepdims=True))
    return centred * lax.rsqrt(spread + norm_epsilon) * norm_gain

def rms_scale(values, norm_gain):
    return values * lax.rsqrt(lax.optimization_barrier(jnp.mean(values * values, axis=-1, keepdims=True)) + norm_epsilon) * norm_gain

def rounded_sum(terms):
    kept = lax.optimization_barrier(terms.astype(jnp.bfloat16))
    return lax.optimization_barrier(jnp.sum(kept.astype(jnp.float32), axis=0))

def grouped_product(left, right):
    row_count = left.shape[0]
    left_groups = left.astype(jnp.float32).reshape(row_count, N_MP, -1)
    right_groups = right.astype(jnp.float32).reshape(N_MP, -1, right.shape[1])
    return jnp.einsum('rgk,gkn->grn', left_groups, right_groups)

def neighbour_table(local_rows, stacked, lists, mesh_patch):
    blocks = [local_rows]
    for number in range(lists.shape[1]):
        source = mesh_patch - offset_of(number)
        usable = jnp.logical_and(source >= 0, source < PATCHES)
        clipped = jnp.clip(source, 0, PATCHES - 1).astype(jnp.int32)
        picked = jnp.take(stacked[clipped], lists[clipped, number], axis=0)
        blocks.append(jnp.where(usable, picked, jnp.zeros_like(picked)))
    return jnp.concatenate(blocks, axis=0)

def reference(grid_in, mesh_static, embed_weight, embed_bias, encode_source, encode_target, encode_edge, encode_bias, encode_out, layer_gain, attention_in, query_gain, key_gain, attention_out, hidden_in, hidden_out, final_gain, decode_node, decode_grid, decode_bias, decode_out, cell_lists, edge_source, edge_target, edge_geometry, halo_lists, neighbours, node_lists, cell_nodes):
    patch_ids = jnp.arange(PATCHES, dtype=jnp.int32)
    grid_latent = jax.nn.silu(jnp.dot(grid_in.T, embed_weight, preferred_element_type=jnp.float32) + embed_bias).astype(jnp.bfloat16)
    projected = jnp.dot(grid_latent, encode_source, preferred_element_type=jnp.float32).astype(jnp.bfloat16)
    band_rows = projected.reshape(PATCHES, G_DEV, D)
    target_part = jnp.dot(mesh_static, encode_target, preferred_element_type=jnp.float32).astype(jnp.bfloat16)
    target_bands = target_part.reshape(PATCHES, M_DEV, D)

    def encode_patch(mesh_patch):
        table = neighbour_table(band_rows[mesh_patch], band_rows, cell_lists, mesh_patch)
        targets = edge_target[mesh_patch]
        source_rows = jnp.take(table, edge_source[mesh_patch], axis=0).astype(jnp.float32)
        target_rows = jnp.take(target_bands[mesh_patch], jnp.minimum(targets, M_DEV - 1), axis=0).astype(jnp.float32)
        geometry_term = jnp.dot(edge_geometry[mesh_patch].T, encode_edge, preferred_element_type=jnp.float32)
        messages = jax.nn.silu(source_rows + target_rows + geometry_term + encode_bias).astype(jnp.bfloat16)
        summed = jax.ops.segment_sum(messages.astype(jnp.float32), targets, num_segments=M_DEV + 1)
        return summed[:M_DEV].astype(jnp.bfloat16)
    gathered = lax.map(encode_patch, patch_ids).reshape(MESH, D)
    latent = mesh_static.astype(jnp.float32) + rounded_sum(grouped_product(gathered, encode_out))
    head_width = query_gain.shape[1]
    for layer_index in range(LAYERS):
        normed = layer_norm(latent, layer_gain[layer_index]).astype(jnp.bfloat16)
        projections = jnp.einsum('rd,dtc->rtc', normed.astype(jnp.float32), attention_in[layer_index].astype(jnp.float32))
        query_matrix = rms_scale(projections[:, 0].reshape(MESH, HEADS, head_width), query_gain[layer_index]).astype(jnp.bfloat16)
        key_rows = rms_scale(projections[:, 1].reshape(MESH, HEADS, head_width), key_gain[layer_index]).astype(jnp.bfloat16)
        value_rows = projections[:, 2].astype(jnp.bfloat16).reshape(MESH, HEADS, head_width)
        key_value = jnp.concatenate([key_rows, value_rows], axis=2).reshape(PATCHES, M_DEV, HEADS, 2 * head_width)
        query_strips = query_matrix.reshape(PATCHES, M_DEV, HEADS, head_width)

        def attend_patch(mesh_patch):
            table = neighbour_table(key_value[mesh_patch], key_value, halo_lists, mesh_patch)
            selected_entries = jnp.take(table, neighbours[mesh_patch], axis=0).astype(jnp.float32)
            attention_logits = jnp.einsum('ave,gave->avg', query_strips[mesh_patch].astype(jnp.float32), selected_entries[..., :head_width]) / math.sqrt(head_width)
            weights = jnp.exp(attention_logits)
            softmax_weights = (weights / lax.optimization_barrier(jnp.sum(weights, axis=-1, keepdims=True))).astype(jnp.bfloat16)
            blended_output = jnp.einsum('rby,yrbg->rbg', softmax_weights.astype(jnp.float32), selected_entries[..., head_width:])
            return blended_output.astype(jnp.bfloat16).reshape(M_DEV, D)
        attended = lax.map(attend_patch, patch_ids).reshape(MESH, D)
        hidden = jax.nn.silu(jnp.dot(normed, hidden_in[layer_index], preferred_element_type=jnp.float32)).astype(jnp.bfloat16)
        partial_terms = grouped_product(attended, attention_out[layer_index]) + grouped_product(hidden, hidden_out[layer_index])
        latent = latent + rounded_sum(partial_terms)
    final_normed = layer_norm(latent, final_gain).astype(jnp.bfloat16)
    node_part = jnp.dot(final_normed, decode_node, preferred_element_type=jnp.float32).astype(jnp.bfloat16).reshape(PATCHES, M_DEV, D)
    latent_bands = grid_latent.reshape(PATCHES, G_DEV, D)
    cell_bands = cell_nodes.reshape(3, PATCHES, G_DEV)

    def decode_patch(mesh_patch):
        table = neighbour_table(node_part[mesh_patch], node_part, node_lists, mesh_patch)
        grid_part = jnp.dot(latent_bands[mesh_patch], decode_grid, preferred_element_type=jnp.float32) + decode_bias
        selected_entries = jnp.take(table, cell_bands[:, mesh_patch], axis=0).astype(jnp.float32)
        return lax.optimization_barrier(jnp.sum(jax.nn.silu(selected_entries + grid_part[None]), axis=0)).astype(jnp.bfloat16)
    activity = lax.map(decode_patch, patch_ids).reshape(GRID, D)
    return rounded_sum(grouped_product(activity, decode_out)).T.astype(jnp.bfloat16)
```

```python
import functools
import math

import jax
import jax.numpy as jnp
from jax import lax
from jax.experimental import pallas as pl
from jax.experimental.pallas import tpu as pltpu
from jax.sharding import PartitionSpec as P

LAYERS = 2
EPSILON = 1e-05
LANES = 128
MESH = pl.DeviceIdType.MESH
BF16 = jnp.bfloat16
F32 = jnp.float32


def offset_of(number):
    return (number // 2 + 1) * (1 if number % 2 == 0 else -1)


def silu(x):
    half = 0.5 * x
    return half + half * jnp.tanh(half)


def dot(a, b):
    return jnp.dot(a, b, preferred_element_type=F32)


def layer_norm(values, gain):
    average = jnp.mean(values, axis=-1, keepdims=True)
    centred = values - average
    spread = jnp.mean(centred * centred, axis=-1, keepdims=True)
    return centred * lax.rsqrt(spread + EPSILON) * gain


def rms_scale(values, gain):
    return values * lax.rsqrt(jnp.mean(values * values, axis=-1, keepdims=True) + EPSILON) * gain


def column(row):
    return jnp.transpose(jnp.broadcast_to(row, (LANES, row.shape[1])))


def fill_one_hot(ref, at, row, first, count):
    col = column(row)
    lane = lax.broadcasted_iota(jnp.int32, col.shape, 1)
    rows = row.shape[1]
    for block in range(count // LANES):
        hit = col == lane + (first + block * LANES)
        ref[at : at + rows, block * LANES : (block + 1) * LANES] = jnp.where(hit, 1.0, 0.0).astype(
            BF16
        )


def kernel(
    patches,
    grid_in,
    mesh_static,
    embed_weight,
    embed_bias,
    encode_source,
    encode_target,
    encode_edge,
    encode_bias,
    encode_out,
    layer_gain,
    attention_in_hbm,
    query_gain,
    key_gain,
    attention_out_hbm,
    hidden_in_hbm,
    hidden_out_hbm,
    final_gain,
    decode_node_hbm,
    decode_grid_hbm,
    decode_bias,
    decode_out,
    cell_lists,
    edge_source,
    edge_target,
    edge_geometry,
    halo_lists,
    neighbours,
    node_lists,
    cell_nodes,
    out,
    attention_in,
    attention_out,
    hidden_in,
    hidden_out,
    decode_node,
    decode_grid,
    latent_grid,
    cell_hot,
    cell_send,
    cell_table,
    source_hot,
    pre,
    node_hot,
    halo_hot,
    counts,
    part_send,
    part_recv,
    half_send,
    half_recv,
    normed,
    latent,
    key_send,
    key_table,
    list_hot,
    node_send,
    node_table,
    choose_hot,
    grid_part,
    out_send,
    out_recv,
    load_sem,
    cell_ssem,
    cell_rsem,
    key_ssem,
    key_rsem,
    node_ssem,
    node_rsem,
    sum_ssem,
    sum_rsem,
    out_ssem,
    out_rsem,
):
    p = lax.axis_index("patch")
    m = lax.axis_index("mp")
    near = cell_lists.shape[1]
    side = m % 2
    sibling = m + 1 - 2 * side
    across = (m + 2) % 4

    loads = [
        pltpu.make_async_copy(src, dst, load_sem.at[i])
        for i, (src, dst) in enumerate(
            [
                (attention_in_hbm, attention_in),
                (hidden_in_hbm, hidden_in),
                (hidden_out_hbm, hidden_out),
                (attention_out_hbm, attention_out),
                (decode_grid_hbm, decode_grid),
                (decode_node_hbm, decode_node),
            ]
        )
    ]
    for load in loads:
        load.start()

    def has_dst(k):
        b = offset_of(k)
        return p + b < patches if b > 0 else p + b >= 0

    def has_src(k):
        b = offset_of(k)
        return p - b >= 0 if b > 0 else p - b < patches

    barrier = pltpu.get_barrier_semaphore()
    for partner in (sibling, across):
        pl.semaphore_signal(barrier, inc=1, device_id={"mp": partner}, device_id_type=MESH)
    for k in range(near):

        @pl.when(has_dst(k))
        def _(k=k):
            pl.semaphore_signal(
                barrier, inc=1, device_id={"patch": p + offset_of(k)}, device_id_type=MESH
            )

    nodes = mesh_static.shape[0]
    cells = latent_grid.shape[0]
    width = encode_source.shape[1]
    cap_cell = cell_lists.shape[2]
    cap_key = halo_lists.shape[2]
    cap_node = node_lists.shape[2]
    half = nodes // 2

    for k in range(near):

        @pl.when(jnp.logical_not(has_src(k)))
        def _(k=k):
            cell_table[k] = jnp.zeros(cell_table.shape[1:], BF16)
            for layer in range(LAYERS):
                key_table[layer, k + 1] = jnp.zeros(key_table.shape[2:], BF16)
            node_table[k + 1] = jnp.zeros(node_table.shape[1:], BF16)

    channel_dims = (((0,), (0,)), ((), ()))
    latent_grid[...] = silu(
        lax.dot_general(grid_in[...], embed_weight[...], channel_dims, preferred_element_type=F32)
        + embed_bias[...][None, :]
    ).astype(BF16)
    projected = dot(latent_grid[...], encode_source[...]).astype(BF16)

    for k in range(near):
        fill_one_hot(cell_hot, k * cap_cell, cell_lists[0, k : k + 1, :], 0, cells)
    cell_send[...] = (
        dot(cell_hot[...], projected).astype(BF16).reshape(near, cap_cell, width)
    )

    peers = 2
    for k in range(near):
        peers = peers + jnp.where(has_src(k), 1, 0)
    pl.semaphore_wait(barrier, peers)

    def passes(send, recv, ssem, rsem):
        return [
            pltpu.make_async_remote_copy(
                src_ref=send(k),
                dst_ref=recv(k),
                send_sem=ssem(k),
                recv_sem=rsem(k),
                device_id={"patch": p + offset_of(k)},
                device_id_type=MESH,
            )
            for k in range(near)
        ]

    def start_all(copies):
        for k in range(near):

            @pl.when(has_dst(k))
            def _(k=k):
                copies[k].start()

    def arrive_all(copies):
        for k in range(near):

            @pl.when(has_src(k))
            def _(k=k):
                copies[k].wait_recv()

    def sent_all(copies):
        for k in range(near):

            @pl.when(has_dst(k))
            def _(k=k):
                copies[k].wait_send()

    cell_copies = passes(
        lambda k: cell_send.at[k],
        lambda k: cell_table.at[k],
        lambda k: cell_ssem.at[k],
        lambda k: cell_rsem.at[k],
    )
    start_all(cell_copies)

    edges = edge_source.shape[1]
    sources = edge_source[0:1, :]
    fill_one_hot(source_hot, 0, sources, 0, source_hot.shape[1])
    targets = edge_target[0:1, :]
    target_part = dot(mesh_static[...], encode_target[...]).astype(BF16)
    geometry_term = lax.dot_general(
        edge_geometry[0], encode_edge[...], channel_dims, preferred_element_type=F32
    )
    fill_one_hot(node_hot, 0, targets, 0, nodes)
    pre[...] = (
        dot(node_hot[...], target_part)
        + geometry_term
        + encode_bias[...][None, :]
        + dot(source_hot[:, :cells], projected)
    )
    gather_hot = jnp.where(
        lax.broadcasted_iota(jnp.int32, (nodes, edges), 0) == targets, 1.0, 0.0
    ).astype(BF16)
    node_rows = lax.broadcasted_iota(jnp.int32, (LANES, nodes), 0)

    arrive_all(cell_copies)
    messages = silu(
        pre[...]
        + dot(source_hot[:, cells:], cell_table[...].reshape(near * cap_cell, width))
    ).astype(BF16)
    gathered = dot(gather_hot, messages).astype(BF16)
    part = dot(gathered, encode_out[...])

    own = pl.multiple_of(side * half, half)
    other = pl.multiple_of((1 - side) * half, half)
    pending = []

    def to_partner(src, dst, at, stage, partner):
        return pltpu.make_async_remote_copy(
            src_ref=src,
            dst_ref=dst,
            send_sem=sum_ssem.at[at, stage],
            recv_sem=sum_rsem.at[at, stage],
            device_id={"mp": partner},
            device_id_type=MESH,
        )

    def add_and_norm(at, part, gain, filler):
        part_send[at] = part.astype(BF16)
        first = to_partner(
            part_send.at[at, pl.ds(other, half)], part_recv.at[at], at, 0, sibling
        )
        first.start()
        first.wait_recv()
        pair = part_send[at, pl.ds(own, half)].astype(F32) + part_recv[at].astype(F32)
        half_send[at] = pair.astype(BF16)
        second = to_partner(half_send.at[at], half_recv.at[at], at, 1, across)
        second.start()
        filler()
        base = mesh_static[pl.ds(own, half)].astype(F32) if at == 0 else latent[...]
        second.wait_recv()
        total = base + (half_send[at].astype(F32) + half_recv[at].astype(F32))
        if at < LAYERS:
            latent[...] = total
        normed[at, pl.ds(own, half)] = layer_norm(total, gain).astype(BF16)
        third = to_partner(
            normed.at[at, pl.ds(own, half)], normed.at[at, pl.ds(own, half)], at, 2, sibling
        )
        third.start()
        back = to_partner(
            normed.at[at, pl.ds(other, half)], normed.at[at, pl.ds(other, half)], at, 2, sibling
        )
        back.wait_recv()
        pending.extend([first, second, third])

    def prepare_attention():
        for k in range(near):
            fill_one_hot(halo_hot, k * cap_key, halo_lists[0, k : k + 1, :], 0, nodes)
        for block in range(counts.shape[1] // LANES):
            total = jnp.zeros((LANES, nodes), F32)
            rows = node_rows + block * LANES
            for n in range(neighbours.shape[1]):
                total = total + jnp.where(rows == neighbours[0, n : n + 1, :], 1.0, 0.0)
            counts[:, block * LANES : (block + 1) * LANES] = jnp.transpose(total)

    def prepare_decode():
        loads[4].wait()
        loads[5].wait()
        grid_part[...] = dot(latent_grid[...], decode_grid[...]) + decode_bias[...][None, :]
        for k in range(near):
            fill_one_hot(list_hot, k * cap_node, node_lists[0, k : k + 1, :], 0, nodes)

    def prepare_choice():
        for j in range(3):
            fill_one_hot(choose_hot, j * cells, cell_nodes[j : j + 1, :], 0, choose_hot.shape[1])

    fillers = [prepare_attention, prepare_decode, prepare_choice]
    add_and_norm(0, part, layer_gain[0:1, :], fillers[0])

    node_copies_key = []
    for layer in range(LAYERS):
        if layer == 0:
            loads[0].wait()
        rows = normed[layer]
        projections = dot(rows, attention_in[layer])
        queries = rms_scale(projections[:, :width], query_gain[layer : layer + 1, :]).astype(BF16)
        keys = rms_scale(projections[:, width : 2 * width], key_gain[layer : layer + 1, :]).astype(
            BF16
        )
        values = projections[:, 2 * width :].astype(BF16)
        key_value = jnp.concatenate([keys, values], axis=1)
        key_send[layer] = (
            dot(halo_hot[...], key_value).astype(BF16).reshape(near, cap_key, 2 * width)
        )
        copies = passes(
            lambda k: key_send.at[layer, k],
            lambda k: key_table.at[layer, k + 1],
            lambda k: key_ssem.at[layer, k],
            lambda k: key_rsem.at[layer, k],
        )
        start_all(copies)
        node_copies_key.append(copies)
        if layer == 0:
            for load in loads[1:4]:
                load.wait()
        hidden = silu(dot(rows, hidden_in[layer])).astype(BF16)
        part = dot(hidden, hidden_out[layer])
        last = (((1,), (1,)), ((), ()))
        scale = 1.0 / math.sqrt(width)
        near_weights = (
            jnp.exp(lax.dot_general(queries, keys, last, preferred_element_type=F32) * scale)
            * counts[:, :nodes]
        )
        arrive_all(copies)
        far = key_table[layer, 1:].reshape(near * cap_key, 2 * width)
        far_weights = (
            jnp.exp(
                lax.dot_general(queries, far[:, :width], last, preferred_element_type=F32) * scale
            )
            * counts[:, nodes:]
        )
        share = 1.0 / (
            jnp.sum(near_weights, axis=1, keepdims=True)
            + jnp.sum(far_weights, axis=1, keepdims=True)
        )
        attended = (
            dot((near_weights * share).astype(BF16), values)
            + dot((far_weights * share).astype(BF16), far[:, width:])
        ).astype(BF16)
        part = part + dot(attended, attention_out[layer])
        gain = layer_gain[layer + 1 : layer + 2, :] if layer + 1 < LAYERS else final_gain[...][None, :]
        add_and_norm(layer + 1, part, gain, fillers[layer + 1])

    node_part = dot(normed[LAYERS], decode_node[...]).astype(BF16)
    node_send[...] = dot(list_hot[...], node_part).astype(BF16).reshape(near, cap_node, width)
    node_copies = passes(
        lambda k: node_send.at[k],
        lambda k: node_table.at[k + 1],
        lambda k: node_ssem.at[k],
        lambda k: node_rsem.at[k],
    )
    start_all(node_copies)
    chosen_near = dot(choose_hot[:, :nodes], node_part)
    arrive_all(node_copies)
    chosen = chosen_near + dot(
        choose_hot[:, nodes:], node_table[1:].reshape(near * cap_node, width)
    )
    activity = silu(chosen[:cells] + grid_part[...])
    for j in range(1, 3):
        activity = activity + silu(chosen[j * cells : (j + 1) * cells] + grid_part[...])
    channels = decode_out.shape[1]
    term = lax.dot_general(
        decode_out[...],
        activity.astype(BF16),
        (((0,), (1,)), ((), ())),
        preferred_element_type=F32,
    )
    padding = out_send.shape[1] - channels
    out_copies = []
    for stage, partner in enumerate((sibling, across)):
        out_send[stage, :channels] = term.astype(BF16)
        if padding:
            out_send[stage, channels:] = jnp.zeros((padding, cells), BF16)
        copy = pltpu.make_async_remote_copy(
            src_ref=out_send.at[stage],
            dst_ref=out_recv.at[stage],
            send_sem=out_ssem.at[stage],
            recv_sem=out_rsem.at[stage],
            device_id={"mp": partner},
            device_id_type=MESH,
        )
        copy.start()
        out_copies.append(copy)
        copy.wait_recv()
        term = out_send[stage, :channels].astype(F32) + out_recv[stage, :channels].astype(F32)
    out[...] = term.astype(BF16)

    for copies in [cell_copies, node_copies] + node_copies_key:
        sent_all(copies)
    for copy in pending + out_copies:
        copy.wait_send()


def shards(patches, *operands):
    operands = list(operands)
    (grid_in, mesh_static, embed_weight) = operands[:3]
    attention_in = operands[10]
    layers, depth, kinds, width = attention_in.shape
    operands[10] = attention_in.reshape(layers, depth, kinds * width)
    attention_out, hidden_in, hidden_out = operands[13:16]
    decode_node, decode_grid = operands[17:19]
    cell_lists, edge_source = operands[21:23]
    halo_lists, neighbours, node_lists, cell_nodes = operands[25:29]
    channels, cells = grid_in.shape
    nodes, features = mesh_static.shape
    near, cap_cell = cell_lists.shape[1:]
    cap_key = halo_lists.shape[2]
    cap_node = node_lists.shape[2]
    edges = edge_source.shape[1]
    half = nodes // 2
    padded = -(-channels // 16) * 16
    sums = layers + 1
    vmem, dma = pltpu.VMEM, pltpu.SemaphoreType.DMA
    scratch = [
        vmem(operands[10].shape, BF16),
        vmem(attention_out.shape, BF16),
        vmem(hidden_in.shape, BF16),
        vmem(hidden_out.shape, BF16),
        vmem(decode_node.shape, BF16),
        vmem(decode_grid.shape, BF16),
        vmem((cells, features), BF16),
        vmem((near * cap_cell, cells), BF16),
        vmem((near, cap_cell, width), BF16),
        vmem((near, cap_cell, width), BF16),
        vmem((edges, cells + near * cap_cell), BF16),
        vmem((edges, width), F32),
        vmem((edges, nodes), BF16),
        vmem((near * cap_key, nodes), BF16),
        vmem((nodes, nodes + near * cap_key), F32),
        vmem((sums, nodes, features), BF16),
        vmem((sums, half, features), BF16),
        vmem((sums, half, features), BF16),
        vmem((sums, half, features), BF16),
        vmem((sums, nodes, features), BF16),
        vmem((half, features), F32),
        vmem((layers, near, cap_key, 2 * width), BF16),
        vmem((layers, near + 1, cap_key, 2 * width), BF16),
        vmem((near * cap_node, nodes), BF16),
        vmem((near, cap_node, width), BF16),
        vmem((near + 1, cap_node, width), BF16),
        vmem((3 * cells, nodes + near * cap_node), BF16),
        vmem((cells, width), F32),
        vmem((2, padded, cells), BF16),
        vmem((2, padded, cells), BF16),
        dma((6,)),
        dma((near,)),
        dma((near,)),
        dma((layers, near)),
        dma((layers, near)),
        dma((near,)),
        dma((near,)),
        dma((sums, 3)),
        dma((sums, 3)),
        dma((2,)),
        dma((2,)),
    ]
    in_hbm = (10, 13, 14, 15, 17, 18)
    return pl.pallas_call(
        functools.partial(kernel, patches),
        out_shape=jax.ShapeDtypeStruct((channels, cells), BF16),
        in_specs=[
            pl.BlockSpec(memory_space=pl.ANY if i in in_hbm else pltpu.VMEM)
            for i in range(len(operands))
        ],
        out_specs=pl.BlockSpec(memory_space=pltpu.VMEM),
        scratch_shapes=scratch,
        compiler_params=pltpu.CompilerParams(
            collective_id=0, has_side_effects=True, vmem_limit_bytes=50 * 1024 * 1024
        ),
        name="denoise",
    )(*operands)


def solution(mesh):
    in_specs = (
        P(None, ("ens", "patch")),
        P("patch", None),
        P(),
        P(),
        P(None, "mp"),
        P(None, "mp"),
        P(None, "mp"),
        P("mp"),
        P("mp", None),
        P(),
        P(None, None, None, "mp"),
        P(),
        P(),
        P(None, "mp", None),
        P(None, None, "mp"),
        P(None, "mp", None),
        P(),
        P(None, "mp"),
        P(None, "mp"),
        P("mp"),
        P("mp", None),
        P("patch", None, None),
        P("patch", None),
        P("patch", None),
        P("patch", None, None),
        P("patch", None, None),
        P("patch", None, None),
        P("patch", None, None),
        P(None, "patch"),
    )
    out_specs = P(None, ("ens", "patch"))
    return jax.shard_map(
        functools.partial(shards, mesh.shape["patch"]),
        mesh=mesh,
        in_specs=in_specs,
        out_specs=out_specs,
        check_vma=False,
    )
```

```python
import functools
import math

import jax
import jax.numpy as jnp
from jax import lax
from jax.experimental import pallas as pl
from jax.experimental.pallas import tpu as pltpu
from jax.sharding import PartitionSpec as P

LAYERS = 2
EPSILON = 1e-05
LANES = 128
MESH = pl.DeviceIdType.MESH
BF16 = jnp.bfloat16
F32 = jnp.float32


def offset_of(number):
    return (number // 2 + 1) * (1 if number % 2 == 0 else -1)


def silu(x):
    half = 0.5 * x
    return half + half * jnp.tanh(half)


def dot(a, b):
    return jnp.dot(a, b, preferred_element_type=F32)


def layer_norm(values, gain):
    average = jnp.mean(values, axis=-1, keepdims=True)
    centred = values - average
    spread = jnp.mean(centred * centred, axis=-1, keepdims=True)
    return centred * lax.rsqrt(spread + EPSILON) * gain


def rms_scale(values, gain):
    return values * lax.rsqrt(jnp.mean(values * values, axis=-1, keepdims=True) + EPSILON) * gain


def column(row):
    return jnp.transpose(jnp.broadcast_to(row, (LANES, row.shape[1])))


def fill_one_hot(ref, at, row, first, count):
    col = column(row)
    lane = lax.broadcasted_iota(jnp.int32, col.shape, 1)
    rows = row.shape[1]
    for block in range(count // LANES):
        hit = col == lane + (first + block * LANES)
        ref[at : at + rows, block * LANES : (block + 1) * LANES] = jnp.where(hit, 1.0, 0.0).astype(
            BF16
        )


NEEDED = (
    (0, 2, 3, 4, 21),
    (22, 23, 1, 5, 24, 6, 7),
    (8, 9, 25, 26),
    (10, 11, 12, 14, 15, 13),
    (18, 19, 27),
    (28, 16, 17, 20),
)


def kernel(patches, count, *refs):
    held, out, local = refs[:count], refs[count], refs[count + 1 : 2 * count + 1]
    load_sem, rest = refs[2 * count + 1], refs[2 * count + 2 :]
    loads = [pltpu.make_async_copy(held[i], local[i], load_sem.at[i]) for i in range(count)]
    for group in NEEDED:
        for i in group:
            loads[i].start()

    def need(number):
        for i in NEEDED[number]:
            loads[i].wait()

    body(patches, need, *local, out, *rest)


def body(
    patches,
    need,
    grid_in,
    mesh_static,
    embed_weight,
    embed_bias,
    encode_source,
    encode_target,
    encode_edge,
    encode_bias,
    encode_out,
    layer_gain,
    attention_in,
    query_gain,
    key_gain,
    attention_out,
    hidden_in,
    hidden_out,
    final_gain,
    decode_node,
    decode_grid,
    decode_bias,
    decode_out,
    cell_lists,
    edge_source,
    edge_target,
    edge_geometry,
    halo_lists,
    neighbours,
    node_lists,
    cell_nodes,
    out,
    latent_grid,
    cell_hot,
    cell_send,
    cell_table,
    source_hot,
    pre,
    node_hot,
    halo_hot,
    counts,
    part_send,
    part_recv,
    half_send,
    half_recv,
    normed,
    latent,
    key_send,
    key_table,
    list_hot,
    node_send,
    node_table,
    choose_hot,
    grid_part,
    out_send,
    out_recv,
    cell_ssem,
    cell_rsem,
    key_ssem,
    key_rsem,
    node_ssem,
    node_rsem,
    sum_ssem,
    sum_rsem,
    out_ssem,
    out_rsem,
):
    p = lax.axis_index("patch")
    m = lax.axis_index("mp")
    near = cell_lists.shape[1]
    side = m % 2
    sibling = m + 1 - 2 * side
    across = (m + 2) % 4

    def has_dst(k):
        b = offset_of(k)
        return p + b < patches if b > 0 else p + b >= 0

    def has_src(k):
        b = offset_of(k)
        return p - b >= 0 if b > 0 else p - b < patches

    barrier = pltpu.get_barrier_semaphore()
    for partner in (sibling, across):
        pl.semaphore_signal(barrier, inc=1, device_id={"mp": partner}, device_id_type=MESH)
    for k in range(near):

        @pl.when(has_dst(k))
        def _(k=k):
            pl.semaphore_signal(
                barrier, inc=1, device_id={"patch": p + offset_of(k)}, device_id_type=MESH
            )

    nodes = mesh_static.shape[0]
    cells = latent_grid.shape[0]
    width = encode_source.shape[1]
    cap_cell = cell_lists.shape[2]
    cap_key = halo_lists.shape[2]
    cap_node = node_lists.shape[2]
    half = nodes // 2

    for k in range(near):

        @pl.when(jnp.logical_not(has_src(k)))
        def _(k=k):
            cell_table[k] = jnp.zeros(cell_table.shape[1:], BF16)
            for layer in range(LAYERS):
                key_table[layer, k + 1] = jnp.zeros(key_table.shape[2:], BF16)
            node_table[k + 1] = jnp.zeros(node_table.shape[1:], BF16)

    need(0)
    channel_dims = (((0,), (0,)), ((), ()))
    latent_grid[...] = silu(
        lax.dot_general(grid_in[...], embed_weight[...], channel_dims, preferred_element_type=F32)
        + embed_bias[...][None, :]
    ).astype(BF16)
    projected = dot(latent_grid[...], encode_source[...]).astype(BF16)

    for k in range(near):
        fill_one_hot(cell_hot, k * cap_cell, cell_lists[0, k : k + 1, :], 0, cells)
    cell_send[...] = (
        dot(cell_hot[...], projected).astype(BF16).reshape(near, cap_cell, width)
    )

    peers = 2
    for k in range(near):
        peers = peers + jnp.where(has_src(k), 1, 0)
    pl.semaphore_wait(barrier, peers)

    def passes(send, recv, ssem, rsem):
        return [
            pltpu.make_async_remote_copy(
                src_ref=send(k),
                dst_ref=recv(k),
                send_sem=ssem(k),
                recv_sem=rsem(k),
                device_id={"patch": p + offset_of(k)},
                device_id_type=MESH,
            )
            for k in range(near)
        ]

    def start_all(copies):
        for k in range(near):

            @pl.when(has_dst(k))
            def _(k=k):
                copies[k].start()

    def arrive_all(copies):
        for k in range(near):

            @pl.when(has_src(k))
            def _(k=k):
                copies[k].wait_recv()

    def sent_all(copies):
        for k in range(near):

            @pl.when(has_dst(k))
            def _(k=k):
                copies[k].wait_send()

    cell_copies = passes(
        lambda k: cell_send.at[k],
        lambda k: cell_table.at[k],
        lambda k: cell_ssem.at[k],
        lambda k: cell_rsem.at[k],
    )
    start_all(cell_copies)

    need(1)
    edges = edge_source.shape[1]
    sources = edge_source[0:1, :]
    fill_one_hot(source_hot, 0, sources, 0, source_hot.shape[1])
    targets = edge_target[0:1, :]
    target_part = dot(mesh_static[...], encode_target[...]).astype(BF16)
    geometry_term = lax.dot_general(
        edge_geometry[0], encode_edge[...], channel_dims, preferred_element_type=F32
    )
    fill_one_hot(node_hot, 0, targets, 0, nodes)
    pre[...] = (
        dot(node_hot[...], target_part)
        + geometry_term
        + encode_bias[...][None, :]
        + dot(source_hot[:, :cells], projected)
    )
    gather_hot = jnp.where(
        lax.broadcasted_iota(jnp.int32, (nodes, edges), 0) == targets, 1.0, 0.0
    ).astype(BF16)
    node_rows = lax.broadcasted_iota(jnp.int32, (LANES, nodes), 0)

    need(2)
    arrive_all(cell_copies)
    messages = silu(
        pre[...]
        + dot(source_hot[:, cells:], cell_table[...].reshape(near * cap_cell, width))
    ).astype(BF16)
    gathered = dot(gather_hot, messages).astype(BF16)
    part = dot(gathered, encode_out[...])

    own = pl.multiple_of(side * half, half)
    other = pl.multiple_of((1 - side) * half, half)
    pending = []

    def to_partner(src, dst, at, stage, partner):
        return pltpu.make_async_remote_copy(
            src_ref=src,
            dst_ref=dst,
            send_sem=sum_ssem.at[at, stage],
            recv_sem=sum_rsem.at[at, stage],
            device_id={"mp": partner},
            device_id_type=MESH,
        )

    def add_and_norm(at, part, gain, filler):
        part_send[at] = part.astype(BF16)
        first = to_partner(
            part_send.at[at, pl.ds(other, half)], part_recv.at[at], at, 0, sibling
        )
        first.start()
        first.wait_recv()
        pair = part_send[at, pl.ds(own, half)].astype(F32) + part_recv[at].astype(F32)
        half_send[at] = pair.astype(BF16)
        second = to_partner(half_send.at[at], half_recv.at[at], at, 1, across)
        second.start()
        filler()
        base = mesh_static[pl.ds(own, half)].astype(F32) if at == 0 else latent[...]
        second.wait_recv()
        total = base + (half_send[at].astype(F32) + half_recv[at].astype(F32))
        if at < LAYERS:
            latent[...] = total
        normed[at, pl.ds(own, half)] = layer_norm(total, gain).astype(BF16)
        third = to_partner(
            normed.at[at, pl.ds(own, half)], normed.at[at, pl.ds(own, half)], at, 2, sibling
        )
        third.start()
        back = to_partner(
            normed.at[at, pl.ds(other, half)], normed.at[at, pl.ds(other, half)], at, 2, sibling
        )
        back.wait_recv()
        pending.extend([first, second, third])

    def prepare_attention():
        for k in range(near):
            fill_one_hot(halo_hot, k * cap_key, halo_lists[0, k : k + 1, :], 0, nodes)
        for block in range(counts.shape[1] // LANES):
            total = jnp.zeros((LANES, nodes), F32)
            rows = node_rows + block * LANES
            for n in range(neighbours.shape[1]):
                total = total + jnp.where(rows == neighbours[0, n : n + 1, :], 1.0, 0.0)
            counts[:, block * LANES : (block + 1) * LANES] = jnp.transpose(total)

    def prepare_decode():
        need(4)
        need(5)
        grid_part[...] = dot(latent_grid[...], decode_grid[...]) + decode_bias[...][None, :]
        for k in range(near):
            fill_one_hot(list_hot, k * cap_node, node_lists[0, k : k + 1, :], 0, nodes)

    def prepare_choice():
        for j in range(3):
            fill_one_hot(choose_hot, j * cells, cell_nodes[j : j + 1, :], 0, choose_hot.shape[1])

    fillers = [prepare_attention, prepare_decode, prepare_choice]
    add_and_norm(0, part, layer_gain[0:1, :], fillers[0])

    node_copies_key = []
    for layer in range(LAYERS):
        if layer == 0:
            need(3)
        rows = normed[layer]
        projections = dot(
            rows, jnp.concatenate([attention_in[layer, kind] for kind in range(3)], axis=1)
        )
        queries = rms_scale(projections[:, :width], query_gain[layer : layer + 1, :]).astype(BF16)
        keys = rms_scale(projections[:, width : 2 * width], key_gain[layer : layer + 1, :]).astype(
            BF16
        )
        values = projections[:, 2 * width :].astype(BF16)
        key_value = jnp.concatenate([keys, values], axis=1)
        key_send[layer] = (
            dot(halo_hot[...], key_value).astype(BF16).reshape(near, cap_key, 2 * width)
        )
        copies = passes(
            lambda k: key_send.at[layer, k],
            lambda k: key_table.at[layer, k + 1],
            lambda k: key_ssem.at[layer, k],
            lambda k: key_rsem.at[layer, k],
        )
        start_all(copies)
        node_copies_key.append(copies)
        hidden = silu(dot(rows, hidden_in[layer])).astype(BF16)
        part = dot(hidden, hidden_out[layer])
        last = (((1,), (1,)), ((), ()))
        scale = 1.0 / math.sqrt(width)
        near_weights = (
            jnp.exp(lax.dot_general(queries, keys, last, preferred_element_type=F32) * scale)
            * counts[:, :nodes]
        )
        arrive_all(copies)
        far = key_table[layer, 1:].reshape(near * cap_key, 2 * width)
        far_weights = (
            jnp.exp(
                lax.dot_general(queries, far[:, :width], last, preferred_element_type=F32) * scale
            )
            * counts[:, nodes:]
        )
        share = 1.0 / (
            jnp.sum(near_weights, axis=1, keepdims=True)
            + jnp.sum(far_weights, axis=1, keepdims=True)
        )
        attended = (
            dot((near_weights * share).astype(BF16), values)
            + dot((far_weights * share).astype(BF16), far[:, width:])
        ).astype(BF16)
        part = part + dot(attended, attention_out[layer])
        gain = layer_gain[layer + 1 : layer + 2, :] if layer + 1 < LAYERS else final_gain[...][None, :]
        add_and_norm(layer + 1, part, gain, fillers[layer + 1])

    node_part = dot(normed[LAYERS], decode_node[...]).astype(BF16)
    node_send[...] = dot(list_hot[...], node_part).astype(BF16).reshape(near, cap_node, width)
    node_copies = passes(
        lambda k: node_send.at[k],
        lambda k: node_table.at[k + 1],
        lambda k: node_ssem.at[k],
        lambda k: node_rsem.at[k],
    )
    start_all(node_copies)
    chosen_near = dot(choose_hot[:, :nodes], node_part)
    arrive_all(node_copies)
    chosen = chosen_near + dot(
        choose_hot[:, nodes:], node_table[1:].reshape(near * cap_node, width)
    )
    activity = silu(chosen[:cells] + grid_part[...])
    for j in range(1, 3):
        activity = activity + silu(chosen[j * cells : (j + 1) * cells] + grid_part[...])
    channels = decode_out.shape[0]
    term = lax.dot_general(
        decode_out[...],
        activity.astype(BF16),
        (((1,), (1,)), ((), ())),
        preferred_element_type=F32,
    )
    padding = out_send.shape[1] - channels
    out_copies = []
    for stage, partner in enumerate((sibling, across)):
        out_send[stage, :channels] = term.astype(BF16)
        if padding:
            out_send[stage, channels:] = jnp.zeros((padding, cells), BF16)
        copy = pltpu.make_async_remote_copy(
            src_ref=out_send.at[stage],
            dst_ref=out_recv.at[stage],
            send_sem=out_ssem.at[stage],
            recv_sem=out_rsem.at[stage],
            device_id={"mp": partner},
            device_id_type=MESH,
        )
        copy.start()
        out_copies.append(copy)
        copy.wait_recv()
        term = out_send[stage, :channels].astype(F32) + out_recv[stage, :channels].astype(F32)
    out[...] = term.astype(BF16)

    for copies in [cell_copies, node_copies] + node_copies_key:
        sent_all(copies)
    for copy in pending + out_copies:
        copy.wait_send()


def shards(patches, *operands):
    operands = list(operands)
    (grid_in, mesh_static, embed_weight) = operands[:3]
    attention_in = operands[10]
    layers, _, _, width = attention_in.shape
    operands[10] = jnp.transpose(attention_in, (0, 2, 1, 3))
    operands[20] = operands[20].T
    cell_lists, edge_source = operands[21:23]
    halo_lists, neighbours, node_lists, cell_nodes = operands[25:29]
    channels, cells = grid_in.shape
    nodes, features = mesh_static.shape
    near, cap_cell = cell_lists.shape[1:]
    cap_key = halo_lists.shape[2]
    cap_node = node_lists.shape[2]
    edges = edge_source.shape[1]
    half = nodes // 2
    padded = -(-channels // 16) * 16
    sums = layers + 1
    vmem, dma = pltpu.VMEM, pltpu.SemaphoreType.DMA
    scratch = [vmem(operand.shape, operand.dtype) for operand in operands]
    scratch += [
        dma((len(operands),)),
        vmem((cells, features), BF16),
        vmem((near * cap_cell, cells), BF16),
        vmem((near, cap_cell, width), BF16),
        vmem((near, cap_cell, width), BF16),
        vmem((edges, cells + near * cap_cell), BF16),
        vmem((edges, width), F32),
        vmem((edges, nodes), BF16),
        vmem((near * cap_key, nodes), BF16),
        vmem((nodes, nodes + near * cap_key), F32),
        vmem((sums, nodes, features), BF16),
        vmem((sums, half, features), BF16),
        vmem((sums, half, features), BF16),
        vmem((sums, half, features), BF16),
        vmem((sums, nodes, features), BF16),
        vmem((half, features), F32),
        vmem((layers, near, cap_key, 2 * width), BF16),
        vmem((layers, near + 1, cap_key, 2 * width), BF16),
        vmem((near * cap_node, nodes), BF16),
        vmem((near, cap_node, width), BF16),
        vmem((near + 1, cap_node, width), BF16),
        vmem((3 * cells, nodes + near * cap_node), BF16),
        vmem((cells, width), F32),
        vmem((2, padded, cells), BF16),
        vmem((2, padded, cells), BF16),
        dma((near,)),
        dma((near,)),
        dma((layers, near)),
        dma((layers, near)),
        dma((near,)),
        dma((near,)),
        dma((sums, 3)),
        dma((sums, 3)),
        dma((2,)),
        dma((2,)),
    ]
    return pl.pallas_call(
        functools.partial(kernel, patches, len(operands)),
        out_shape=jax.ShapeDtypeStruct((channels, cells), BF16),
        in_specs=[pl.BlockSpec(memory_space=pltpu.HBM)] * len(operands),
        out_specs=pl.BlockSpec(memory_space=pltpu.VMEM),
        scratch_shapes=scratch,
        compiler_params=pltpu.CompilerParams(
            collective_id=0, has_side_effects=True, vmem_limit_bytes=64 * 1024 * 1024
        ),
        name="denoise",
    )(*operands)


def solution(mesh):
    in_specs = (
        P(None, ("ens", "patch")),
        P("patch", None),
        P(),
        P(),
        P(None, "mp"),
        P(None, "mp"),
        P(None, "mp"),
        P("mp"),
        P("mp", None),
        P(),
        P(None, None, None, "mp"),
        P(),
        P(),
        P(None, "mp", None),
        P(None, None, "mp"),
        P(None, "mp", None),
        P(),
        P(None, "mp"),
        P(None, "mp"),
        P("mp"),
        P("mp", None),
        P("patch", None, None),
        P("patch", None),
        P("patch", None),
        P("patch", None, None),
        P("patch", None, None),
        P("patch", None, None),
        P("patch", None, None),
        P(None, "patch"),
    )
    out_specs = P(None, ("ens", "patch"))
    return jax.shard_map(
        functools.partial(shards, mesh.shape["patch"]),
        mesh=mesh,
        in_specs=in_specs,
        out_specs=out_specs,
        check_vma=False,
    )
```
